768 devices in a mesh: row: 64 (over y, x, core), col: 12 (over z).
Axes of the slice: x: 4, y: 8, z: 12, core: 2. Of those that a mesh axis runs over, the one named last changes fastest.
Arguments:
- a_tiles: bfloat16 [256, 24, 128, 128], P('row', 'col'), may hold values from -28 to 28
- block_owner: int32 [256, 24], P('row', 'col'), may hold values from 0 to 63, as said below
- send_rows: int32 [64, 64], replicated, may hold values from 0 to 3
- stripe: bfloat16 [32768, 3072], P('row', 'col'), may hold values from -0.109375 to 0.109375
Outputs:
- inflated: float32 [32768, 3072], P('row', 'col')
The draws below stay inside these ranges and needn't reach their ends.
Inputs may be any that keep to these rules, and one draw needn't show every extreme that they name: `block_owner`: each value names an index along row.
All inputs are finite; a program needn't handle non-finite values.
Results may differ from the reference program's by a relative error of at most 0.0003.
Values may be sent and summed in bfloat16 or wider, within the bound.
A program may use at most 64 MiB of HBM per device.

```python
import jax
import jax.numpy as jnp
from jax import lax

TILE = 128
TR = 4
KSLOT = 24
NT = 256
STRIPE = 3072


def draw_a_tiles(key, part):
    key = jax.random.fold_in(key, 3)
    keys = jax.random.split(key, 2)
    shape = (NT, KSLOT, TILE, TILE)
    devices = NT // TR
    position = (jnp.arange(NT, dtype=jnp.int32) // TR).astype(jnp.float32)
    ramp = position / max(devices - 1, 1)
    base = jnp.clip(jax.random.normal(keys[0], shape), -5.0, 5.0)
    level = 1.0 + 2.0 * ramp
    row_scale = jnp.exp(jax.random.uniform(keys[1], (NT, 1, TILE, 1), minval=0.0, maxval=1.15))
    return (base * row_scale * jnp.sqrt(level)[:, None, None, None]).astype(jnp.bfloat16)


def draw_block_owner(key, part):
    key = jax.random.fold_in(key, 7)
    owner_count = NT // TR
    keys = jax.random.split(key, 6)
    popular = jax.random.randint(keys[0], (owner_count,), 0, 8) ** 2
    noise = jax.random.randint(keys[1], (owner_count, owner_count), 0, 1024)
    score = (popular[None, :] * 1024 + noise) * owner_count + jnp.arange(owner_count, dtype=jnp.int32)[None, :]
    ranked = jnp.argsort(-score, axis=1).astype(jnp.int32)
    live_count = jax.random.randint(keys[2], (owner_count,), max(1, owner_count // 2), owner_count + 1)
    full_device = jax.random.randint(keys[3], (), 0, owner_count)
    live_count = jnp.where(jnp.arange(owner_count, dtype=jnp.int32) == full_device, owner_count, live_count)
    device_of = jnp.arange(NT, dtype=jnp.int32) // TR
    limit = live_count[device_of][:, None]
    first = jax.random.randint(keys[4], (NT, KSLOT), 0, 65536) % limit
    second = jax.random.randint(keys[5], (NT, KSLOT), 0, 65536) % limit
    chosen = jnp.minimum(first, second)
    return jnp.take_along_axis(ranked[device_of], chosen, axis=1).astype(jnp.int32)


def with_ends(array, rng, smallest, high):
    longest = array.shape.index(max(array.shape))
    spots = []
    for shift in (0, 1):
        where = [jax.random.randint(jax.random.fold_in(rng, axis), (), 0, length) for axis, length in enumerate(array.shape)]
        where[longest] = (where[longest] + shift) % array.shape[longest]
        spots.append(tuple(where))
    return array.at[spots[0]].set(smallest).at[spots[1]].set(high)


def shard_levels(own_key, shape, pieces, smallest, largest):
    gain, own = 1.0, jax.random.fold_in(own_key, 6)
    for dim, shards_of in pieces:
        steps = jnp.exp(jax.random.uniform(jax.random.fold_in(own, dim), (shards_of,), jnp.float32, smallest / len(pieces), largest / len(pieces)))
        gain = gain * jnp.repeat(steps, shape[dim] // shards_of).reshape([-1 if axis == dim else 1 for axis in range(len(shape))])
    return gain


def normal_values(key, shape, width, most, cuts=(), kind=jnp.bfloat16):
    drawn = jax.random.normal(key, shape, jnp.float32) * width
    if len(cuts) > 0:
        drawn = shard_levels(key, shape, cuts, -0.22, 0.18) * drawn
    return jnp.clip(drawn, min=-most, max=most).astype(kind)


def setup_inputs(seed: int = 0) -> dict:
    seeds = jax.random.split(jax.random.key(seed), 5)
    a_tiles = draw_a_tiles(jax.random.fold_in(seeds[4], 71), 0)
    block_owner = draw_block_owner(jax.random.fold_in(seeds[4], 71), 0)
    send_rows = with_ends(jax.random.randint(seeds[2], (NT // TR, NT // TR), 0, TR), jax.random.fold_in(seeds[2], 1), 0, TR - 1).astype(jnp.int32)
    stripe = normal_values(seeds[3], (NT * TILE, STRIPE), (KSLOT * TILE) ** -0.5, 0.109375, ((0, 64), (1, 12)))
    return {"a_tiles": a_tiles, "block_owner": block_owner, "send_rows": send_rows, "stripe": stripe}


def reference(a_tiles, block_owner, send_rows, stripe):
    stripe_tiles = stripe.reshape(NT, TILE, STRIPE)
    device_of = jnp.arange(NT, dtype=jnp.int32) // TR
    positions = (block_owner * TR + send_rows[block_owner, device_of[:, None]]).astype(jnp.int32)

    def tile_row(inputs):
        left_tiles, row_positions = inputs
        right_tiles = stripe_tiles[row_positions]
        return jnp.einsum("sab,sbw->aw", left_tiles.astype(jnp.float32), right_tiles.astype(jnp.float32))

    product = lax.map(tile_row, (a_tiles, positions))
    squared = product * product
    column_sum = jnp.sum(squared, axis=(0, 1))
    return ((NT * TILE) * squared / column_sum).reshape(NT * TILE, STRIPE)
```

```python
import functools

import jax
import jax.numpy as jnp
from jax import lax
from jax.experimental import pallas as pl
from jax.experimental.pallas import tpu as pltpu
from jax.sharding import PartitionSpec as P

MESH = pl.DeviceIdType.MESH
NX, NY, NC = 4, 8, 2
FIRST = 32


def hops_of(n):
    return [(+1, 0, n // 2), (-1, 1, n // 2), (+1, 1, n // 2 - 1), (-1, 0, n // 2 - 1)]


def place_of(direction, hop, n):
    return hop if direction > 0 or hop == n // 2 else n // 2 + hop


def distance_of(place, n):
    return place if place <= n // 2 else -(place - n // 2)


def kernel(nz, a_ref, owner_ref, rows_ref, stripe_ref, out_ref, rows, ids_out, ids, ids_s, held, sent1, got1, sent2,
           got2, sums1, sums2, ysem, yrecv, zsem, zrecv, isem, irecv, xsem, xrecv, s1, r1, s2, r2, c1, d1, c2, d2,
           local_sem, *blocks):
    yb, xb = blocks[:NY], blocks[NY:]
    me, z = lax.axis_index("row"), lax.axis_index("col")
    y, x, c = me // (NX * NC), (me // NC) % NX, me % NC

    def row(dy, dx, dc):
        return ((y + dy + NY) % NY) * (NX * NC) + ((x + dx + NX) % NX) * NC + (c + dc) % NC

    def at(dy=0, dx=0, dc=0, dz=0):
        return (row(dy, dx, dc), (z + dz + nz) % nz)

    tiles, edge, width = stripe_ref.shape
    rest = edge - FIRST
    xg = [(dx, dc) for dx in range(NX) for dc in range(NC) if dx or dc]
    yg = [(dy, dc) for dy in range(NY) for dc in range(NC) if dy or dc]

    own = [
        pltpu.make_async_copy(rows_ref, rows, local_sem.at[0]),
        pltpu.make_async_copy(stripe_ref.at[:, pl.ds(FIRST, rest)], yb[0], local_sem.at[1]),
        pltpu.make_async_copy(stripe_ref.at[:, pl.ds(0, FIRST)], xb[0], local_sem.at[2]),
        pltpu.make_async_copy(a_ref, held.at[0], local_sem.at[3]),
    ]
    for copy in own:
        copy.start()
    ids_out[...] = jnp.zeros_like(ids_out)
    ids_out[0 : owner_ref.shape[0], 0 : owner_ref.shape[1]] = owner_ref[...]
    ids[0] = ids_out[...]

    barrier = pltpu.get_barrier_semaphore()
    met = [(0, dx, dc, 0) for dx, dc in xg] + [(dy, 0, dc, 0) for dy, dc in yg] + [(0, 0, 0, 1), (0, 0, 0, -1)]
    for dy, dx, dc, dz in met:
        pl.semaphore_signal(barrier, inc=1, device_id=at(-dy, -dx, dc, -dz), device_id_type=MESH)
    pl.semaphore_wait(barrier, len(met))

    started = []

    def send(src, dst, send_sem, recv_sem, device):
        copy = pltpu.make_async_remote_copy(
            src_ref=src, dst_ref=dst, send_sem=send_sem, recv_sem=recv_sem, device_id=device, device_id_type=MESH
        )
        copy.start()
        started.append(copy)
        return copy

    half = tiles // 2
    arriving = {}

    def y_send(lane, hop):
        direction, chunk, _ = hops_of(NY)[lane]
        part = pl.ds(chunk * half, half)
        if hop == 0:
            src = stripe_ref.at[part, pl.ds(FIRST, rest)]
        else:
            src = yb[place_of(direction, hop, NY)].at[part]
        arriving["y", lane, hop + 1] = send(
            src, yb[place_of(direction, hop + 1, NY)].at[part], ysem.at[lane, hop], yrecv.at[lane, hop],
            at(dy=direction))

    def z_send(lane, hop):
        direction, chunk, _ = hops_of(nz)[lane]
        part = pl.ds(chunk * half, half)
        src = a_ref.at[part] if hop == 0 else held.at[place_of(direction, hop, nz), part]
        arriving["z", lane, hop + 1] = send(
            src, held.at[place_of(direction, hop + 1, nz), part], zsem.at[lane, hop], zrecv.at[lane, hop],
            at(dz=direction))

    def i_send(lane, hop):
        direction = hops_of(nz)[lane][0]
        src = ids_out if hop == 0 else ids.at[place_of(direction, hop, nz)]
        arriving["i", lane, hop + 1] = send(
            src, ids.at[place_of(direction, hop + 1, nz)], isem.at[lane, hop], irecv.at[lane, hop], at(dz=direction))

    def last(kind, lane):
        if kind == "i":
            return nz // 2 if lane == 0 else nz // 2 - 1
        return hops_of(NY if kind == "y" else nz)[lane][2]

    senders = {"y": y_send, "z": z_send, "i": i_send}

    def arrive(kind, lane, hop):
        if hop <= last(kind, lane):
            arriving[kind, lane, hop].wait_recv()
            if hop < last(kind, lane):
                senders[kind](lane, hop)

    def give1(place):
        block = yb[place]
        dy = -distance_of(place, NY)
        owner = row(dy, 0, 0)
        for n, (dx, dc) in enumerate(xg):
            slot = place * len(xg) + n
            sent1[slot] = block[rows[owner, row(0, dx, dc)]]
            pltpu.make_async_remote_copy(
                src_ref=sent1.at[slot], dst_ref=got1.at[owner], send_sem=s1, recv_sem=r1, device_id=at(0, dx, dc),
                device_id_type=MESH).start()
        got1[owner] = block[rows[owner, me]]

    def from_x(dx, dc=0):
        return y * (NX * NC) + ((x + dx + NX) % NX) * NC + (c + dc) % NC

    def slot2(yy, xx, cc):
        return (yy * NC + cc) * NX + xx

    def give2():
        for n, (dy, dc) in enumerate(yg):
            there = row(dy, 0, dc)
            for dx in range(NX):
                xx = (x + dx) % NX
                sent2[n * NX + xx] = xb[dx][rows[from_x(dx), there]]
            pltpu.make_async_remote_copy(
                src_ref=sent2.at[pl.ds(n * NX, NX)], dst_ref=got2.at[pl.ds(slot2(y, 0, c), NX)], send_sem=s2,
                recv_sem=r2, device_id=at(dy, 0, dc), device_id_type=MESH).start()
        for dx in range(NX):
            got2[slot2(y, (x + dx) % NX, c)] = xb[dx][rows[from_x(dx), me]]

    for lane in range(4):
        y_send(lane, 0)
        z_send(lane, 0)
    x_sent = [
        send(stripe_ref.at[:, pl.ds(0, FIRST)], xb[dx], xsem.at[dx - 1], xrecv.at[dx - 1], at(dx=-dx))
        for dx in range(1, NX)
    ]
    i_send(0, 0)
    i_send(1, 0)
    for copy in own:
        copy.wait()
    give1(0)
    for hop in range(1, nz // 2 + 1):
        for pair in (0, 2):
            for kind in ("y", "z") if hop <= NY // 2 else ("z",):
                for lane in (pair, pair + 1):
                    arrive(kind, lane, hop)
        arrive("i", 0, hop)
        arrive("i", 1, hop)
        if hop < NY // 2:
            give1(place_of(1, hop, NY))
            give1(place_of(-1, hop, NY))
        elif hop == NY // 2:
            give1(hop)
        if hop == 1:
            for copy in x_sent:
                copy.wait_recv()
            give2()

    copy = pltpu.make_async_copy(ids, ids_s, local_sem.at[4])
    copy.start()
    copy.wait()
    n1, n2 = NY * len(xg), len(yg) * NX
    pltpu.make_async_copy(got1.at[pl.ds(0, n1)], got1.at[pl.ds(0, n1)], r1).wait()
    pltpu.make_async_copy(got2.at[pl.ds(0, n2)], got2.at[pl.ds(0, n2)], r2).wait()

    def multiply(p, total):
        acc = jnp.zeros((edge, width), jnp.float32)
        for h in range(nz):
            parts = []
            for s in range(2):
                o = ids_s[h, p, s]
                parts += [got2[slot2(o // (NX * NC), (o // NC) % NX, o % NC)], got1[o]]
            left = jnp.concatenate([held[h, p, 0], held[h, p, 1]], axis=1)
            acc += jnp.dot(left, jnp.concatenate(parts, axis=0), preferred_element_type=jnp.float32)
        squared = acc * acc
        out_ref[p] = squared
        return total + jnp.sum(squared.reshape(edge // 8, 8, width), axis=0)

    total = lax.fori_loop(0, tiles, multiply, jnp.zeros((8, width), jnp.float32))

    sums1[0] = total
    copies = [
        send(sums1.at[0], sums1.at[n + 1], c1.at[n], d1.at[n], at(0, dx, dc)) for n, (dx, dc) in enumerate(xg)
    ]
    for copy in copies:
        copy.wait_recv()
    sums2[0] = jnp.sum(sums1[...], axis=0)
    copies = [send(sums2.at[0], sums2.at[dy], c2.at[dy - 1], d2.at[dy - 1], at(dy)) for dy in range(1, NY)]
    for copy in copies:
        copy.wait_recv()
    column_sum = jnp.sum(jnp.sum(sums2[...], axis=0), axis=0, keepdims=True)

    row_count = float(NY * NX * NC * tiles * edge)

    def scale(p, _):
        out_ref[p] = row_count * out_ref[p] / column_sum
        return 0

    lax.fori_loop(0, tiles, scale, 0)
    for copy in started:
        copy.wait_send()
    pltpu.make_async_copy(sent1, sent1, s1).wait()
    pltpu.make_async_copy(sent2, sent2, s2).wait()


def solution(mesh):
    nz = mesh.shape["col"]
    n_xg, n_yg = NX * NC - 1, NY * NC - 1

    def local(a_tiles, block_owner, send_rows, stripe):
        tiles, slots, edge, _ = a_tiles.shape
        width = stripe.shape[1]
        rest = edge - FIRST
        vmem, any_ = pl.BlockSpec(memory_space=pltpu.VMEM), pl.BlockSpec(memory_space=pl.ANY)
        dma, bf16 = pltpu.SemaphoreType.DMA, jnp.bfloat16
        out = pl.pallas_call(
            functools.partial(kernel, nz),
            out_shape=jax.ShapeDtypeStruct((tiles, edge, width), jnp.float32),
            in_specs=[any_, vmem, any_, any_],
            out_specs=vmem,
            scratch_shapes=[
                pltpu.SMEM(send_rows.shape, jnp.int32),
                pltpu.VMEM((8, 128), jnp.int32),
                pltpu.VMEM((nz, 8, 128), jnp.int32),
                pltpu.SMEM((nz, 8, 128), jnp.int32),
                pltpu.VMEM((nz, tiles, slots, edge, edge), bf16),
                pltpu.VMEM((NY * n_xg, rest, width), bf16),
                pltpu.VMEM((NY * NX * NC, rest, width), bf16),
                pltpu.VMEM((n_yg * NX, FIRST, width), bf16),
                pltpu.VMEM((NY * NX * NC, FIRST, width), bf16),
                pltpu.VMEM((n_xg + 1, 8, width), jnp.float32),
                pltpu.VMEM((NY, 8, width), jnp.float32),
                dma((4, NY // 2)), dma((4, NY // 2)),
                dma((4, nz // 2)), dma((4, nz // 2)),
                dma((2, nz // 2)), dma((2, nz // 2)),
                dma((NX - 1,)), dma((NX - 1,)),
                dma, dma, dma, dma,
                dma((n_xg,)), dma((n_xg,)),
                dma((NY - 1,)), dma((NY - 1,)),
                dma((5,)),
            ]
            + [pltpu.VMEM((tiles, rest, width), bf16)] * NY
            + [pltpu.VMEM((tiles, FIRST, width), bf16)] * NX,
            compiler_params=pltpu.CompilerParams(
                collective_id=0, has_side_effects=True, vmem_limit_bytes=40 * 2**20
            ),
            name="expand",
        )(a_tiles, block_owner, send_rows, stripe.reshape(tiles, edge, width))
        return out.reshape(tiles * edge, width)

    placed = (P("row", "col", None, None), P("row", "col"), P(), P("row", "col"))
    return jax.shard_map(local, mesh=mesh, in_specs=placed, out_specs=P("row", "col"), check_vma=False)
```

```python
import functools

import jax
import jax.numpy as jnp
from jax import lax
from jax.experimental import pallas as pl
from jax.experimental.pallas import tpu as pltpu
from jax.sharding import PartitionSpec as P

MESH = pl.DeviceIdType.MESH
VMEM = 60 * 2**20
NX, NY, NC = 4, 8, 2
EARLY = 4
FIRST = 32


def hops_of(n):
    return [(+1, 0, n // 2), (-1, 1, n // 2), (+1, 1, n // 2 - 1), (-1, 0, n // 2 - 1)]


def place_of(direction, hop, n):
    return hop if direction > 0 or hop == n // 2 else n // 2 + hop


def distance_of(place, n):
    return place if place <= n // 2 else -(place - n // 2)


def kernel(nz, a_ref, owner_ref, rows_ref, stripe_ref, out_ref, rows, owners, ids_out, ids, ids_s, held, sent1, got1,
           sent2, got2, sums1, sums2, ysem, yrecv, zsem, zrecv, isem, irecv, xsem, xrecv, s1, r1, s2, r2, c1, d1, c2, d2,
           local_sem, plane_in, ring_in, *blocks):
    yb, xb = blocks[:NY], blocks[NY:]
    me, z = lax.axis_index("row"), lax.axis_index("col")
    y, x, c = me // (NX * NC), (me // NC) % NX, me % NC

    def row(dy, dx, dc):
        return ((y + dy + NY) % NY) * (NX * NC) + ((x + dx + NX) % NX) * NC + (c + dc) % NC

    def at(dy=0, dx=0, dc=0, dz=0):
        return (row(dy, dx, dc), (z + dz + nz) % nz)

    tiles, edge, width = stripe_ref.shape
    rest = edge - FIRST
    xg = [(dx, dc) for dx in (2, 1, 3, 0) for dc in range(NC) if dx or dc]
    yg = [(dy, dc) for dy in (4, 3, 5, 2, 6, 1, 7, 0) for dc in range(NC) if dy or dc]

    own = [
        pltpu.make_async_copy(rows_ref, rows, local_sem.at[0]),
        pltpu.make_async_copy(stripe_ref.at[:, pl.ds(FIRST, rest)], yb[0], local_sem.at[1]),
        pltpu.make_async_copy(stripe_ref.at[:, pl.ds(0, FIRST)], xb[0], local_sem.at[2]),
        pltpu.make_async_copy(a_ref, held.at[0], local_sem.at[3]),
        pltpu.make_async_copy(owner_ref, owners, local_sem.at[4]),
    ]
    for copy in own:
        copy.start()

    barrier = pltpu.get_barrier_semaphore()

    def tell(dz, dy, dx, core):
        there = ((y + dy + NY) % NY) * (NX * NC) + ((x + dx + NX) % NX) * NC + core
        pl.semaphore_signal(barrier, inc=1, device_id=(there, (z + dz + nz) % nz), device_id_type=MESH)

    plane = [(dy, 0) for dy in range(1, NY)] + [(0, dx) for dx in range(1, NX)]
    for dy, dx in plane:
        tell(0, dy, dx, 0)
    tell(1, 0, 0, 1)
    tell(-1, 0, 0, 1)

    @pl.when(c == 1)
    def _():
        tell(0, 0, 0, 0)

    ids_out[...] = jnp.zeros_like(ids_out)
    own.pop().wait()
    ids_out[0 : owners.shape[0], 0 : owners.shape[1]] = owners[...]
    ids[0] = ids_out[...]

    @pl.when(c == 0)
    def _():
        pl.semaphore_wait(barrier, 2 * len(plane) + 1)
        pl.semaphore_signal(plane_in, inc=1, device_id=at(dc=1), device_id_type=MESH)

    @pl.when(c == 1)
    def _():
        pl.semaphore_wait(plane_in, 1)

    def meet_ring():
        @pl.when(c == 1)
        def _():
            pl.semaphore_wait(barrier, 4)
            pl.semaphore_signal(ring_in, inc=1, device_id=at(dc=1), device_id_type=MESH)

        @pl.when(c == 0)
        def _():
            pl.semaphore_wait(ring_in, 1)

    def remote(src, dst, send_sem, recv_sem, device):
        return pltpu.make_async_remote_copy(
            src_ref=src, dst_ref=dst, send_sem=send_sem, recv_sem=recv_sem, device_id=device, device_id_type=MESH
        )

    half = tiles // 2

    def y_copy(lane, hop):
        direction, chunk, _ = hops_of(NY)[lane]
        part = pl.ds(chunk * half, half)
        if hop == 0:
            src = stripe_ref.at[part, pl.ds(FIRST, rest)]
        else:
            src = yb[place_of(direction, hop, NY)].at[part]
        dst = yb[place_of(direction, hop + 1, NY)].at[part]
        return remote(src, dst, ysem, yrecv.at[lane, hop], at(dy=direction))

    def z_copy(lane, hop):
        direction, chunk, _ = hops_of(nz)[lane]
        part = pl.ds(chunk * half, half)
        src = a_ref.at[part] if hop == 0 else held.at[place_of(direction, hop, nz), part]
        dst = held.at[place_of(direction, hop + 1, nz), part]
        return remote(src, dst, zsem, zrecv.at[lane, hop], at(dz=direction))

    def i_copy(lane, hop):
        direction = hops_of(nz)[lane][0]
        src = ids_out if hop == 0 else ids.at[place_of(direction, hop, nz)]
        dst = ids.at[place_of(direction, hop + 1, nz)]
        return remote(src, dst, isem, irecv.at[lane, hop], at(dz=direction))

    def arrive(copy_of, lane, hop, last):
        if hop <= last:
            copy_of(lane, hop - 1).wait_recv()
            if hop < last:
                copy_of(lane, hop).start()

    def give1(place):
        block = yb[place]
        owner = row(-distance_of(place, NY), 0, 0)
        for n, (dx, dc) in enumerate(xg):
            slot = place * len(xg) + n
            sent1[slot] = block[rows[owner, row(0, dx, dc)]]
            remote(sent1.at[slot], got1.at[owner], s1, r1, at(0, dx, dc)).start()
        got1[owner] = block[rows[owner, me]]

    def from_x(dx):
        return row(0, dx, 0)

    def slot2(yy, xx, cc):
        return (yy * NC + cc) * NX + xx

    def give2(first, stop):
        for n, (dy, dc) in list(enumerate(yg))[max(first, 0) : max(stop, 0)]:
            there = row(dy, 0, dc)
            for dx in range(NX):
                sent2[n * NX + (x + dx) % NX] = xb[dx][rows[from_x(dx), there]]
            remote(sent2.at[pl.ds(n * NX, NX)], got2.at[pl.ds(slot2(y, 0, c), NX)], s2, r2, at(dy, 0, dc)).start()

    def x_copy(dx):
        return remote(stripe_ref.at[:, pl.ds(0, FIRST)], xb[dx], xsem, xrecv.at[dx - 1], at(dx=-dx))

    def start_ring():
        meet_ring()
        for lane in range(4):
            z_copy(lane, 0).start()
        i_copy(0, 0).start()
        i_copy(1, 0).start()

    def y_step(hop):
        for lane in range(4):
            arrive(y_copy, lane, hop, hops_of(NY)[lane][2])

    def z_step(hop):
        for lane in range(4):
            arrive(z_copy, lane, hop, hops_of(nz)[lane][2])
        for lane in range(2):
            arrive(i_copy, lane, hop, nz // 2 - lane)

    def x_step():
        for dx in range(1, NX):
            x_copy(dx).wait_recv()
        for dx in range(NX):
            got2[slot2(y, (x + dx) % NX, c)] = xb[dx][rows[from_x(dx), me]]

    for lane in range(4):
        y_copy(lane, 0).start()
    for dx in range(1, NX):
        x_copy(dx).start()

    def run(start, offset):
        if start == 0:
            start_ring()
        for copy in own:
            copy.wait()
        give1(0)
        done = 0
        for hop in range(1, NY // 2 + 1):
            y_step(hop)
            if start == hop:
                start_ring()
            if hop > offset:
                done += 1
                z_step(done)
            if hop == 2:
                x_step()
            give2(5 * hop - 10, 5 * hop - 5)
            give1(place_of(1, hop, NY))
            if hop < NY // 2:
                give1(place_of(-1, hop, NY))
        for hop in range(done + 1, nz // 2 + 1):
            z_step(hop)

    @pl.when(z == 0)
    def _():
        run(1, 1)

    @pl.when((z > 0) & (z < EARLY))
    def _():
        run(1, 1)

    @pl.when(z >= EARLY)
    def _():
        run(0, 0)

    copy = pltpu.make_async_copy(ids, ids_s, local_sem.at[4])
    copy.start()
    copy.wait()
    n1, n2 = NY * len(xg), len(yg) * NX
    pltpu.make_async_copy(got2.at[pl.ds(0, n2)], got2.at[pl.ds(0, n2)], r2).wait()
    pltpu.make_async_copy(got1.at[pl.ds(0, n1)], got1.at[pl.ds(0, n1)], r1).wait()

    def multiply(p, total):
        acc = jnp.zeros((edge, width), jnp.float32)
        for h in range(nz):
            parts = []
            for s in range(2):
                o = ids_s[h, s, p]
                parts += [got2[slot2(o // (NX * NC), (o // NC) % NX, o % NC)], got1[o]]
            left = jnp.concatenate([held[h, p, 0], held[h, p, 1]], axis=1)
            acc += jnp.dot(left, jnp.concatenate(parts, axis=0), preferred_element_type=jnp.float32)
        squared = acc * acc
        out_ref[p] = squared
        return total + jnp.sum(squared.reshape(edge // 8, 8, width), axis=0)

    total = lax.fori_loop(0, tiles, multiply, jnp.zeros((8, width), jnp.float32))

    sums1[0] = total
    for n, (dx, dc) in enumerate(xg):
        remote(sums1.at[0], sums1.at[n + 1], c1, d1, at(0, dx, dc)).start()
    pltpu.make_async_copy(sums1.at[pl.ds(1, len(xg))], sums1.at[pl.ds(1, len(xg))], d1).wait()
    sums2[0] = jnp.sum(sums1[...], axis=0)
    for dy in (4, 3, 5, 2, 6, 1, 7):
        remote(sums2.at[0], sums2.at[dy], c2, d2, at(dy)).start()
    pltpu.make_async_copy(sums2.at[pl.ds(1, NY - 1)], sums2.at[pl.ds(1, NY - 1)], d2).wait()
    column_sum = jnp.sum(jnp.sum(sums2[...], axis=0), axis=0, keepdims=True)
    row_count = float(NY * NX * NC * tiles * edge)

    def scale(p, _):
        out_ref[p] = row_count * out_ref[p] / column_sum
        return 0

    lax.fori_loop(0, tiles, scale, 0)

    for ref, sem in (
        (sent1, s1), (sent2, s2), (sums1.at[pl.ds(1, len(xg))], c1), (sums2.at[pl.ds(1, NY - 1)], c2),
        (sent1.at[pl.ds(0, (NY - 1) * tiles)], ysem), (sent2.at[pl.ds(0, (NX - 1) * tiles)], xsem),
        (held.at[pl.ds(1, nz - 1)], zsem), (ids.at[pl.ds(1, nz - 1)], isem),
    ):
        pltpu.make_async_copy(ref, ref, sem).wait()


def solution(mesh):
    nz = mesh.shape["col"]
    n_xg, n_yg = NX * NC - 1, NY * NC - 1

    def local(a_tiles, block_owner, send_rows, stripe):
        tiles, slots, edge, _ = a_tiles.shape
        width = stripe.shape[1]
        rest = edge - FIRST
        vmem, hbm = pl.BlockSpec(memory_space=pltpu.VMEM), pl.BlockSpec(memory_space=pltpu.MemorySpace.HBM)
        dma, bf16 = pltpu.SemaphoreType.DMA, jnp.bfloat16
        out = pl.pallas_call(
            functools.partial(kernel, nz),
            out_shape=jax.ShapeDtypeStruct((tiles, edge, width), jnp.float32),
            in_specs=[hbm, hbm, hbm, hbm],
            out_specs=vmem,
            scratch_shapes=[
                pltpu.SMEM(send_rows.shape, jnp.int32),
                pltpu.VMEM((slots, tiles), jnp.int32),
                pltpu.VMEM((8, 128), jnp.int32),
                pltpu.VMEM((nz, 8, 128), jnp.int32),
                pltpu.SMEM((nz, 8, 128), jnp.int32),
                pltpu.VMEM((nz, tiles, slots, edge, edge), bf16),
                pltpu.VMEM((NY * n_xg, rest, width), bf16),
                pltpu.VMEM((NY * NX * NC, rest, width), bf16),
                pltpu.VMEM((n_yg * NX, FIRST, width), bf16),
                pltpu.VMEM((NY * NX * NC, FIRST, width), bf16),
                pltpu.VMEM((n_xg + 1, 8, width), jnp.float32),
                pltpu.VMEM((NY, 8, width), jnp.float32),
                dma, dma((4, NY // 2)),
                dma, dma((4, nz // 2)),
                dma, dma((2, nz // 2)),
                dma, dma((NX - 1,)),
                dma, dma, dma, dma, dma, dma, dma, dma,
                dma((5,)),
                pltpu.SemaphoreType.REGULAR,
                pltpu.SemaphoreType.REGULAR,
            ]
            + [pltpu.VMEM((tiles, rest, width), bf16)] * NY
            + [pltpu.VMEM((tiles, FIRST, width), bf16)] * NX,
            compiler_params=pltpu.CompilerParams(
                collective_id=0, has_side_effects=True, vmem_limit_bytes=VMEM
            ),
            name="expand",
        )(a_tiles, block_owner.T, send_rows, stripe.reshape(tiles, edge, width))
        return out.reshape(tiles * edge, width)

    placed = (P("row", "col", None, None), P("row", "col"), P(), P("row", "col"))
    return jax.shard_map(local, mesh=mesh, in_specs=placed, out_specs=P("row", "col"), check_vma=False)
```

```python
import functools

import jax
import jax.numpy as jnp
from jax import lax
from jax.experimental import pallas as pl
from jax.experimental.pallas import tpu as pltpu
from jax.sharding import PartitionSpec as P

MESH = pl.DeviceIdType.MESH
FIRST_PLANE = (
    "o u Y1 y1", "g1 s Y2 w", "r y2 g2 Z1", "x t0 z1 t1", "Y3 y3 Z2 g3", "z2 t2 Z3 Y4",
    "g4 z3 t3 Z4", "z4 Z5 z5",
)
EARLY_PLANES = (
    "o u s Y1", "y1 w r g1", "Y2 Z1 y2 z1", "g2 x t0 Z2", "Y3 t1 y3 z2", "g3 t2 Z3 Y4",
    "z3 g4 Z4 t3", "z4 Z5 z5",
)
LATE_PLANES = (
    "s o u w", "r Y1 Z1 y1", "z1 g1 Y2 Z2", "y2 z2 g2 x", "t0 Z3 Y3 t1", "y3 z3 g3 t2",
    "Z4 Y4 z4 g4", "Z5 t3 z5",
)
VMEM = 62 * 2**20
NX, NY, NC = 4, 8, 2
EARLY = 4
FIRST = 32


def hops_of(n):
    return [(+1, 0, n // 2), (-1, 1, n // 2), (+1, 1, n // 2 - 1), (-1, 0, n // 2 - 1)]


def ring_of(n):
    return [(+1, 0, n // 2 - 1), (-1, 1, n // 2), (+1, 1, n // 2 - 1), (-1, 0, n // 2)]


def place_of(direction, hop, n):
    return hop if direction > 0 or hop == n // 2 else n // 2 + hop


def distance_of(place, n):
    return place if place <= n // 2 else -(place - n // 2)


def kernel(nz, a_ref, owner_ref, rows_ref, stripe_ref, out_ref, rows, owners, ids_out, ids, ids_s, held, sent1, got1,
           sent2, got2, sums1, sums2, ysem, yrecv, zsem, zfirst, zrecv, isem, irecv, xsem, xrecv, s1, r1, s2, r2, c1, d1, c2, d2,
           local_sem, plane_in, ring_in, *blocks):
    yb, xb = blocks[:NY], blocks[NY:]
    me, z = lax.axis_index("row"), lax.axis_index("col")
    y, x, c = lax.div(me, NX * NC), lax.rem(lax.div(me, NC), NX), lax.rem(me, NC)

    def row(dy, dx, dc):
        return lax.rem(y + (dy + NY), NY) * (NX * NC) + lax.rem(x + (dx + NX), NX) * NC + lax.rem(c + dc, NC)

    def at(dy=0, dx=0, dc=0, dz=0):
        return (row(dy, dx, dc), lax.rem(z + (dz + nz), nz) if dz else z)

    tiles, edge, width = stripe_ref.shape
    rest = edge - FIRST
    xg = [(dx, dc) for dx in (2, 1, 3, 0) for dc in range(NC) if dx or dc]
    yg = [(dy, dc) for dy in (0, 1, 7, 2, 6, 3, 5, 4) for dc in range(NC) if dy or dc]

    own = [
        pltpu.make_async_copy(rows_ref, rows, local_sem.at[0]),
        pltpu.make_async_copy(stripe_ref.at[:, pl.ds(FIRST, rest)], yb[0], local_sem.at[1]),
        pltpu.make_async_copy(stripe_ref.at[:, pl.ds(0, FIRST)], xb[0], local_sem.at[2]),
        pltpu.make_async_copy(a_ref, held.at[0], local_sem.at[3]),
        pltpu.make_async_copy(owner_ref, owners, local_sem.at[4]),
    ]
    for copy in own:
        copy.start()

    barrier = pltpu.get_barrier_semaphore()

    def tell(dz, dy, dx, core):
        there, level = at(dy, dx, 0, dz)
        pl.semaphore_signal(barrier, inc=1, device_id=(there - c + core, level), device_id_type=MESH)

    plane = [(1, 0), (-1, 0)] + [(0, dx) for dx in range(1, NX)]
    for dy, dx in plane:
        tell(0, dy, dx, 0)
    tell(1, 0, 0, 1)
    tell(-1, 0, 0, 1)

    @pl.when(c == 1)
    def _():
        tell(0, 0, 0, 0)

    ids_out[...] = jnp.zeros_like(ids_out)
    own.pop().wait()
    ids_out[0 : owners.shape[0], 0 : owners.shape[1]] = owners[...]
    ids[0] = ids_out[...]

    @pl.when(c == 0)
    def _():
        pl.semaphore_wait(barrier, 2 * len(plane) + 1)
        pl.semaphore_signal(plane_in, inc=1, device_id=at(dc=1), device_id_type=MESH)

    @pl.when(c == 1)
    def _():
        pl.semaphore_wait(plane_in, 1)

    def meet_ring():
        @pl.when(c == 1)
        def _():
            pl.semaphore_wait(barrier, 4)
            pl.semaphore_signal(ring_in, inc=1, device_id=at(dc=1), device_id_type=MESH)

        @pl.when(c == 0)
        def _():
            pl.semaphore_wait(ring_in, 1)

    def remote(src, dst, send_sem, recv_sem, device):
        return pltpu.make_async_remote_copy(
            src_ref=src, dst_ref=dst, send_sem=send_sem, recv_sem=recv_sem, device_id=device, device_id_type=MESH
        )

    half = tiles // 2

    def y_copy(lane, hop):
        direction, chunk, _ = hops_of(NY)[lane]
        part = pl.ds(chunk * half, half)
        if hop == 0:
            src = stripe_ref.at[part, pl.ds(FIRST, rest)]
        else:
            src = yb[place_of(direction, hop, NY)].at[part]
        dst = yb[place_of(direction, hop + 1, NY)].at[part]
        return remote(src, dst, ysem, yrecv.at[lane, hop], at(dy=direction))

    def z_copy(lane, hop):
        direction, chunk, _ = ring_of(nz)[lane]
        part = pl.ds(chunk * half, half)
        src = a_ref.at[part] if hop == 0 else held.at[place_of(direction, hop, nz), part]
        dst = held.at[place_of(direction, hop + 1, nz), part]
        return remote(src, dst, zfirst if hop == 0 and lane < 2 else zsem, zrecv.at[lane, hop], at(dz=direction))

    def i_copy(lane, hop):
        direction = ring_of(nz)[lane][0]
        src = ids_out if hop == 0 else ids.at[place_of(direction, hop, nz)]
        dst = ids.at[place_of(direction, hop + 1, nz)]
        return remote(src, dst, isem, irecv.at[lane, hop], at(dz=direction))

    def arrive(copy_of, lane, hop, last):
        if hop <= last:
            copy_of(lane, hop - 1).wait_recv()
            if hop < last:
                copy_of(lane, hop).start()

    def slot1(k):
        return jnp.where(k > NY // 2, 2 * (NY - k), jnp.maximum(2 * k - 1, 0))

    def give1(hop):
        places = [place_of(1, hop, NY)] + ([place_of(-1, hop, NY)] if 0 < hop < NY // 2 else [])
        first = max(2 * hop - 1, 0)
        owners_y = [row(-distance_of(place, NY), 0, 0) for place in places]
        mine = (x * NC + c) * NY + first
        for n, (dx, dc) in enumerate(xg):
            there = row(0, dx, dc)
            for k, (place, owner) in enumerate(zip(places, owners_y)):
                sent1[n * NY + first + k] = yb[place][rows[owner, there]]
            remote(sent1.at[pl.ds(n * NY + first, len(places))], got1.at[pl.ds(mine, len(places))], s1, r1,
                   at(0, dx, dc)).start()
        for k, (place, owner) in enumerate(zip(places, owners_y)):
            got1[mine + k] = yb[place][rows[owner, me]]

    def from_x(dx):
        return row(0, dx, 0)

    def slot2(yy, xx, cc):
        return (yy * NC + cc) * NX + xx

    def give2(first, stop):
        for n, (dy, dc) in list(enumerate(yg))[first:stop]:
            there = row(dy, 0, dc)
            for dx in range(NX):
                sent2[n * NX + lax.rem(x + dx, NX)] = xb[dx][rows[from_x(dx), there]]
            remote(sent2.at[pl.ds(n * NX, NX)], got2.at[pl.ds(slot2(y, 0, c), NX)], s2, r2, at(dy, 0, dc)).start()

    def x_copy(dx):
        return remote(stripe_ref.at[:, pl.ds(0, FIRST)], xb[dx], xsem, xrecv.at[dx - 1], at(dx=-dx))

    def start_ring():
        meet_ring()
        for lane in range(2):
            i_copy(lane, 0).start()
            z_copy(lane, 0).start()

    def y_step(hop, second):
        for lane in (2, 3) if second else (0, 1):
            arrive(y_copy, lane, hop, hops_of(NY)[lane][2])

    def z_step(hop, second):
        for lane in (2, 3) if second else (0, 1):
            last = ring_of(nz)[lane][2]
            if hop <= last:
                z_copy(lane, hop - 1).wait_recv()
            if not second:
                arrive(i_copy, lane, hop, nz // 2 - 1 + lane)
            if hop < last:
                z_copy(lane, hop).start()

    def x_step():
        for dx in range(1, NX):
            x_copy(dx).wait_recv()
        for dx in range(NX):
            got2[slot2(y, lax.rem(x + dx, NX), c)] = xb[dx][rows[from_x(dx), me]]

    for lane in range(2):
        y_copy(lane, 0).start()
    for dx in range(1, NX):
        x_copy(dx).start()

    def run(order):
        for step in [step for part in order for step in part.split()]:
            kind, n = step[0], int(step[1:] or 0)
            if kind == "s":
                start_ring()
            elif kind == "w":
                pltpu.make_async_copy(held.at[0], held.at[0], zfirst).wait()
            elif kind == "r":
                z_copy(2, 0).start()
                z_copy(3, 0).start()
            elif kind == "u":
                y_copy(2, 0).start()
                y_copy(3, 0).start()
            elif kind == "o":
                for copy in own:
                    copy.wait()
                give1(0)
            elif kind in "Yy":
                y_step(n, kind == "y")
            elif kind in "Zz":
                z_step(n, kind == "z")
            elif kind == "x":
                x_step()
            elif kind == "t":
                give2(*((0, 5), (5, 9), (9, 13), (13, 15))[n])
            elif kind == "g":
                give1(n)

    @pl.when(z == 0)
    def _():
        run(FIRST_PLANE)

    @pl.when((z > 0) & (z < EARLY))
    def _():
        run(EARLY_PLANES)

    @pl.when(z >= EARLY)
    def _():
        run(LATE_PLANES)

    n1, n2 = NY * len(xg), len(yg) * NX
    far = nz // 2
    near = [pltpu.make_async_copy(ids.at[h], ids_s.at[h], local_sem.at[h]) for h in range(nz) if h != far]
    for copy in near:
        copy.start()
    for copy in near:
        copy.wait()
    pltpu.make_async_copy(got2.at[pl.ds(0, n2)], got2.at[pl.ds(0, n2)], r2).wait()
    pltpu.make_async_copy(got1.at[pl.ds(0, n1)], got1.at[pl.ds(0, n1)], r1).wait()

    def partial(p, blocks_of_a):
        acc = jnp.zeros((edge, width), jnp.float32)
        for h in blocks_of_a:
            parts = []
            for s in range(2):
                o = ids_s[h, s, p]
                oy, ox, oc = o >> 3, (o >> 1) & 3, o & 1
                parts += [got2[slot2(oy, ox, oc)], got1[(ox * NC + oc) * NY + slot1((y - oy) & (NY - 1))]]
            left = jnp.concatenate([held[h, p, 0], held[h, p, 1]], axis=1)
            acc += jnp.dot(left, jnp.concatenate(parts, axis=0), preferred_element_type=jnp.float32)
        return acc

    def most(p, _):
        out_ref[p] = partial(p, [h for h in range(nz) if h != far])
        return 0

    lax.fori_loop(0, tiles, most, 0)
    i_copy(1, far - 1).wait_recv()
    copy = pltpu.make_async_copy(ids.at[far], ids_s.at[far], local_sem.at[far])
    copy.start()
    for lane in (1, 3):
        z_copy(lane, far - 1).wait_recv()
    copy.wait()

    def finish(p, total):
        acc = out_ref[p] + partial(p, [far])
        squared = acc * acc
        out_ref[p] = squared
        return total + jnp.sum(squared.reshape(edge // 8, 8, width), axis=0)

    total = lax.fori_loop(0, tiles, finish, jnp.zeros((8, width), jnp.float32))

    sums1[0] = jnp.sum(total, axis=0, keepdims=True)
    for n, (dx, dc) in enumerate(xg):
        remote(sums1.at[0], sums1.at[n + 1], c1, d1, at(0, dx, dc)).start()
    pltpu.make_async_copy(sums1.at[pl.ds(1, len(xg))], sums1.at[pl.ds(1, len(xg))], d1).wait()
    sums2[0] = jnp.sum(sums1[...], axis=0)
    for dy in (4, 3, 5, 2, 6, 1, 7):
        remote(sums2.at[0], sums2.at[dy], c2, d2, at(dy)).start()
    pltpu.make_async_copy(sums2.at[pl.ds(1, NY - 1)], sums2.at[pl.ds(1, NY - 1)], d2).wait()
    column_sum = jnp.sum(sums2[...], axis=0)
    row_count = float(NY * NX * NC * tiles * edge)

    def scale(p, _):
        out_ref[p] = row_count * out_ref[p] / column_sum
        return 0

    lax.fori_loop(0, tiles, scale, 0)

    for ref, sem in (
        (sent1, s1), (sent2, s2), (sums1.at[pl.ds(1, len(xg))], c1), (sums2.at[pl.ds(1, NY - 1)], c2),
        (sent1.at[pl.ds(0, (NY - 1) * tiles)], ysem), (sent2.at[pl.ds(0, (NX - 1) * tiles)], xsem),
        (held.at[pl.ds(1, nz - 2)], zsem), (ids.at[pl.ds(1, nz - 1)], isem),
    ):
        pltpu.make_async_copy(ref, ref, sem).wait()


def solution(mesh):
    nz = mesh.shape["col"]
    n_xg, n_yg = NX * NC - 1, NY * NC - 1

    def local(a_tiles, block_owner, send_rows, stripe):
        tiles, slots, edge, _ = a_tiles.shape
        width = stripe.shape[1]
        rest = edge - FIRST
        vmem, hbm = pl.BlockSpec(memory_space=pltpu.VMEM), pl.BlockSpec(memory_space=pltpu.MemorySpace.HBM)
        dma, bf16 = pltpu.SemaphoreType.DMA, jnp.bfloat16
        out = pl.pallas_call(
            functools.partial(kernel, nz),
            out_shape=pltpu.VMEM((tiles, edge, width), jnp.float32),
            in_specs=[hbm, hbm, hbm, hbm],
            out_specs=vmem,
            scratch_shapes=[
                pltpu.SMEM(send_rows.shape, jnp.int32),
                pltpu.VMEM((slots, tiles), jnp.int32),
                pltpu.VMEM((8, 128), jnp.int32),
                pltpu.VMEM((nz, 8, 128), jnp.int32),
                pltpu.SMEM((nz, 8, 128), jnp.int32),
                pltpu.VMEM((nz, tiles, slots, edge, edge), bf16),
                pltpu.VMEM((NY * n_xg, rest, width), bf16),
                pltpu.VMEM((NY * NX * NC, rest, width), bf16),
                pltpu.VMEM((n_yg * NX, FIRST, width), bf16),
                pltpu.VMEM((NY * NX * NC, FIRST, width), bf16),
                pltpu.VMEM((n_xg + 1, 1, width), jnp.float32),
                pltpu.VMEM((NY, 1, width), jnp.float32),
                dma, dma((4, NY // 2)),
                dma, dma, dma((4, nz // 2)),
                dma, dma((2, nz // 2)),
                dma, dma((NX - 1,)),
                dma, dma, dma, dma, dma, dma, dma, dma,
                dma((nz,)),
                pltpu.SemaphoreType.REGULAR,
                pltpu.SemaphoreType.REGULAR,
            ]
            + [pltpu.VMEM((tiles, rest, width), bf16)] * NY
            + [pltpu.VMEM((tiles, FIRST, width), bf16)] * NX,
            compiler_params=pltpu.CompilerParams(
                collective_id=0, has_side_effects=True, vmem_limit_bytes=VMEM
            ),
            name="expand",
        )(a_tiles, block_owner.T, send_rows, stripe.reshape(tiles, edge, width))
        return out.reshape(tiles * edge, width)

    placed = (P("row", "col", None, None), P("row", "col"), P(), P("row", "col"))
    return jax.shard_map(local, mesh=mesh, in_specs=placed, out_specs=P("row", "col"), check_vma=False)
```

```python
import functools

import jax
import jax.numpy as jnp
from jax import lax
from jax.experimental import pallas as pl
from jax.experimental.pallas import tpu as pltpu
from jax.sharding import PartitionSpec as P

MESH = pl.DeviceIdType.MESH
FIRST_PLANE = (
    "o u Y1 y1", "g1 s r Y2", "y2 w g2 Z1", "x t0 z1 t1", "Y3 y3 Z2 g3", "z2 t2 Z3 Y4",
    "g4 z3 t3 Z4", "z4 Z5 z5",
)
EARLY_PLANES = (
    "o u s r", "Y1 y1 g1 w", "Y2 Z1 y2 z1", "g2 x t0 Z2", "Y3 t1 y3 z2", "g3 t2 Z3 Y4",
    "z3 g4 Z4 t3", "z4 Z5 z5",
)
LATE_PLANES = (
    "s o u r", "Y1 Z1 y1 z1", "g1 w Y2 Z2", "y2 z2 g2 x", "t0 Z3 Y3 t1", "y3 z3 g3 t2",
    "Z4 Y4 z4 g4", "Z5 t3 z5",
)
VMEM = 62 * 2**20
NX, NY, NC = 4, 8, 2
EARLY = 4
FIRST = 32


def hops_of(n):
    return [(+1, 0, n // 2), (-1, 1, n // 2), (+1, 1, n // 2 - 1), (-1, 0, n // 2 - 1)]


def ring_of(n):
    return [(+1, 0, n // 2 - 1), (-1, 1, n // 2), (+1, 1, n // 2 - 1), (-1, 0, n // 2)]


def place_of(direction, hop, n):
    return hop if direction > 0 or hop == n // 2 else n // 2 + hop


def distance_of(place, n):
    return place if place <= n // 2 else -(place - n // 2)


def kernel(nz, a_ref, owner_ref, rows_ref, stripe_ref, out_ref, rows, owners, ids_out, ids, ids_s, held, sent1, got1,
           sent2, got2, sums1, sums2, ysem, yrecv, zsem, zfirst, zrecv, isem, irecv, xsem, xrecv, s1, r1, s2, r2, c1, d1, c2, d2,
           local_sem, plane_in, ring_in, *blocks):
    yb, xb = blocks[:NY], blocks[NY:]
    me, z = lax.axis_index("row"), lax.axis_index("col")
    y, x, c = lax.div(me, NX * NC), lax.rem(lax.div(me, NC), NX), lax.rem(me, NC)

    def row(dy, dx, dc):
        return lax.rem(y + (dy + NY), NY) * (NX * NC) + lax.rem(x + (dx + NX), NX) * NC + lax.rem(c + dc, NC)

    def at(dy=0, dx=0, dc=0, dz=0):
        return (row(dy, dx, dc), lax.rem(z + (dz + nz), nz) if dz else z)

    tiles, edge, width = stripe_ref.shape
    rest = edge - FIRST
    xg = [(dx, dc) for dx in (2, 1, 3, 0) for dc in range(NC) if dx or dc]
    yg = [(dy, dc) for dy in (0, 1, 7, 2, 6, 3, 5, 4) for dc in range(NC) if dy or dc]

    own = [
        pltpu.make_async_copy(rows_ref, rows, local_sem.at[0]),
        pltpu.make_async_copy(stripe_ref.at[:, pl.ds(FIRST, rest)], yb[0], local_sem.at[1]),
        pltpu.make_async_copy(stripe_ref.at[:, pl.ds(0, FIRST)], xb[0], local_sem.at[2]),
        pltpu.make_async_copy(a_ref, held.at[0], local_sem.at[3]),
        pltpu.make_async_copy(owner_ref, owners, local_sem.at[4]),
    ]
    for copy in own:
        copy.start()

    barrier = pltpu.get_barrier_semaphore()

    def tell(dz, dy, dx, core):
        there, level = at(dy, dx, 0, dz)
        pl.semaphore_signal(barrier, inc=1, device_id=(there - c + core, level), device_id_type=MESH)

    plane = [(1, 0), (-1, 0)] + [(0, dx) for dx in range(1, NX)]
    for dy, dx in plane:
        tell(0, dy, dx, 0)
    tell(1, 0, 0, 1)
    tell(-1, 0, 0, 1)

    @pl.when(c == 1)
    def _():
        tell(0, 0, 0, 0)

    ids_out[...] = jnp.zeros_like(ids_out)
    own.pop().wait()
    ids_out[0 : owners.shape[0], 0 : owners.shape[1]] = owners[...]
    ids[0] = ids_out[...]

    @pl.when(c == 0)
    def _():
        pl.semaphore_wait(barrier, 2 * len(plane) + 1)
        pl.semaphore_signal(plane_in, inc=1, device_id=at(dc=1), device_id_type=MESH)

    @pl.when(c == 1)
    def _():
        pl.semaphore_wait(plane_in, 1)

    def meet_ring():
        @pl.when(c == 1)
        def _():
            pl.semaphore_wait(barrier, 4)
            pl.semaphore_signal(ring_in, inc=1, device_id=at(dc=1), device_id_type=MESH)

        @pl.when(c == 0)
        def _():
            pl.semaphore_wait(ring_in, 1)

    def remote(src, dst, send_sem, recv_sem, device):
        return pltpu.make_async_remote_copy(
            src_ref=src, dst_ref=dst, send_sem=send_sem, recv_sem=recv_sem, device_id=device, device_id_type=MESH
        )

    half = tiles // 2

    def y_copy(lane, hop):
        direction, chunk, _ = hops_of(NY)[lane]
        part = pl.ds(chunk * half, half)
        if hop == 0:
            src = stripe_ref.at[part, pl.ds(FIRST, rest)]
        else:
            src = yb[place_of(direction, hop, NY)].at[part]
        dst = yb[place_of(direction, hop + 1, NY)].at[part]
        return remote(src, dst, ysem, yrecv.at[lane, hop], at(dy=direction))

    def z_copy(lane, hop):
        direction, chunk, _ = ring_of(nz)[lane]
        part = pl.ds(chunk * half, half)
        src = a_ref.at[part] if hop == 0 else held.at[place_of(direction, hop, nz), part]
        dst = held.at[place_of(direction, hop + 1, nz), part]
        return remote(src, dst, zfirst if hop == 0 and lane < 2 else zsem, zrecv.at[lane, hop], at(dz=direction))

    def i_copy(lane, hop):
        direction = ring_of(nz)[lane][0]
        src = ids_out if hop == 0 else ids.at[place_of(direction, hop, nz)]
        dst = ids.at[place_of(direction, hop + 1, nz)]
        return remote(src, dst, isem, irecv.at[lane, hop], at(dz=direction))

    def arrive(copy_of, lane, hop, last):
        if hop <= last:
            copy_of(lane, hop - 1).wait_recv()
            if hop < last:
                copy_of(lane, hop).start()

    def slot1(k):
        return jnp.where(k > NY // 2, 2 * (NY - k), jnp.maximum(2 * k - 1, 0))

    def give1(hop):
        places = [place_of(1, hop, NY)] + ([place_of(-1, hop, NY)] if 0 < hop < NY // 2 else [])
        first = max(2 * hop - 1, 0)
        owners_y = [row(-distance_of(place, NY), 0, 0) for place in places]
        mine = (x * NC + c) * NY + first
        for n, (dx, dc) in enumerate(xg):
            there = row(0, dx, dc)
            for k, (place, owner) in enumerate(zip(places, owners_y)):
                sent1[n * NY + first + k] = yb[place][rows[owner, there]]
            remote(sent1.at[pl.ds(n * NY + first, len(places))], got1.at[pl.ds(mine, len(places))], s1, r1,
                   at(0, dx, dc)).start()
        for k, (place, owner) in enumerate(zip(places, owners_y)):
            got1[mine + k] = yb[place][rows[owner, me]]

    def from_x(dx):
        return row(0, dx, 0)

    def slot2(yy, xx, cc):
        return (yy * NC + cc) * NX + xx

    def give2(first, stop):
        for n, (dy, dc) in list(enumerate(yg))[first:stop]:
            there = row(dy, 0, dc)
            for dx in range(NX):
                sent2[n * NX + lax.rem(x + dx, NX)] = xb[dx][rows[from_x(dx), there]]
            remote(sent2.at[pl.ds(n * NX, NX)], got2.at[pl.ds(slot2(y, 0, c), NX)], s2, r2, at(dy, 0, dc)).start()

    def x_copy(dx):
        return remote(stripe_ref.at[:, pl.ds(0, FIRST)], xb[dx], xsem, xrecv.at[dx - 1], at(dx=-dx))

    def start_ring():
        meet_ring()
        for lane in range(2):
            i_copy(lane, 0).start()
            z_copy(lane, 0).start()

    def y_step(hop, second):
        for lane in (2, 3) if second else (0, 1):
            arrive(y_copy, lane, hop, hops_of(NY)[lane][2])

    def z_step(hop, second):
        for lane in (2, 3) if second else (0, 1):
            last = ring_of(nz)[lane][2]
            if hop <= last:
                z_copy(lane, hop - 1).wait_recv()
            if not second:
                arrive(i_copy, lane, hop, nz // 2 - 1 + lane)
            if hop < last:
                z_copy(lane, hop).start()

    def x_step():
        for dx in range(1, NX):
            x_copy(dx).wait_recv()
        for dx in range(NX):
            got2[slot2(y, lax.rem(x + dx, NX), c)] = xb[dx][rows[from_x(dx), me]]

    for lane in range(2):
        y_copy(lane, 0).start()
    for dx in range(1, NX):
        x_copy(dx).start()

    def run(order):
        for step in [step for part in order for step in part.split()]:
            kind, n = step[0], int(step[1:] or 0)
            if kind == "s":
                start_ring()
            elif kind == "w":
                pltpu.make_async_copy(held.at[0], held.at[0], zfirst).wait()
            elif kind == "r":
                z_copy(2, 0).start()
                z_copy(3, 0).start()
            elif kind == "u":
                y_copy(2, 0).start()
                y_copy(3, 0).start()
            elif kind == "o":
                for copy in own:
                    copy.wait()
                give1(0)
            elif kind in "Yy":
                y_step(n, kind == "y")
            elif kind in "Zz":
                z_step(n, kind == "z")
            elif kind == "x":
                x_step()
            elif kind == "t":
                give2(*((0, 5), (5, 9), (9, 13), (13, 15))[n])
            elif kind == "g":
                give1(n)

    @pl.when(z == 0)
    def _():
        run(FIRST_PLANE)

    @pl.when((z > 0) & (z < EARLY))
    def _():
        run(EARLY_PLANES)

    @pl.when(z >= EARLY)
    def _():
        run(LATE_PLANES)

    n1, n2 = NY * len(xg), len(yg) * NX
    far = nz // 2
    near = [pltpu.make_async_copy(ids.at[h], ids_s.at[h], local_sem.at[h]) for h in range(nz) if h != far]
    for copy in near:
        copy.start()
    for copy in near:
        copy.wait()
    pltpu.make_async_copy(got2.at[pl.ds(0, n2)], got2.at[pl.ds(0, n2)], r2).wait()
    pltpu.make_async_copy(got1.at[pl.ds(0, n1)], got1.at[pl.ds(0, n1)], r1).wait()

    def partial(p, blocks_of_a):
        acc = jnp.zeros((edge, width), jnp.float32)
        for h in blocks_of_a:
            parts = []
            for s in range(2):
                o = ids_s[h, s, p]
                oy, ox, oc = o >> 3, (o >> 1) & 3, o & 1
                parts += [got2[slot2(oy, ox, oc)], got1[(ox * NC + oc) * NY + slot1((y - oy) & (NY - 1))]]
            left = jnp.concatenate([held[h, p, 0], held[h, p, 1]], axis=1)
            acc += jnp.dot(left, jnp.concatenate(parts, axis=0), preferred_element_type=jnp.float32)
        return acc

    def most(p, _):
        out_ref[p] = partial(p, [h for h in range(nz) if h != far])
        return 0

    lax.fori_loop(0, tiles, most, 0)
    i_copy(1, far - 1).wait_recv()
    copy = pltpu.make_async_copy(ids.at[far], ids_s.at[far], local_sem.at[far])
    copy.start()
    for lane in (1, 3):
        z_copy(lane, far - 1).wait_recv()
    copy.wait()

    def finish(p, total):
        acc = out_ref[p] + partial(p, [far])
        squared = acc * acc
        out_ref[p] = squared
        return total + jnp.sum(squared.reshape(edge // 8, 8, width), axis=0)

    total = lax.fori_loop(0, tiles, finish, jnp.zeros((8, width), jnp.float32))

    sums1[0] = jnp.sum(total, axis=0, keepdims=True)
    far_first = sorted(
        ((dy, dx, dc) for dy in range(NY) for dx in range(NX) for dc in range(NC) if dy or dx or dc),
        key=lambda o: -min(o[0], NY - o[0]) - min(o[1], NX - o[1]),
    )
    for n, (dy, dx, dc) in enumerate(far_first):
        remote(sums1.at[0], sums1.at[n + 1], c1, d1, at(dy, dx, dc)).start()
    pltpu.make_async_copy(sums1.at[pl.ds(1, len(far_first))], sums1.at[pl.ds(1, len(far_first))], d1).wait()
    column_sum = jnp.sum(sums1[...], axis=0)
    row_count = float(NY * NX * NC * tiles * edge)

    def scale(p, _):
        out_ref[p] = row_count * out_ref[p] / column_sum
        return 0

    lax.fori_loop(0, tiles, scale, 0)

    for ref, sem in (
        (sent1, s1), (sent2, s2), (sums1.at[pl.ds(1, len(far_first))], c1),
        (sent1.at[pl.ds(0, (NY - 1) * tiles)], ysem), (sent2.at[pl.ds(0, (NX - 1) * tiles)], xsem),
        (held.at[pl.ds(1, nz - 2)], zsem), (ids.at[pl.ds(1, nz - 1)], isem),
    ):
        pltpu.make_async_copy(ref, ref, sem).wait()


def solution(mesh):
    nz = mesh.shape["col"]
    n_xg, n_yg = NX * NC - 1, NY * NC - 1

    def local(a_tiles, block_owner, send_rows, stripe):
        tiles, slots, edge, _ = a_tiles.shape
        width = stripe.shape[1]
        rest = edge - FIRST
        vmem, hbm = pl.BlockSpec(memory_space=pltpu.VMEM), pl.BlockSpec(memory_space=pltpu.MemorySpace.HBM)
        dma, bf16 = pltpu.SemaphoreType.DMA, jnp.bfloat16
        out = pl.pallas_call(
            functools.partial(kernel, nz),
            out_shape=pltpu.VMEM((tiles, edge, width), jnp.float32),
            in_specs=[hbm, hbm, hbm, hbm],
            out_specs=vmem,
            scratch_shapes=[
                pltpu.SMEM(send_rows.shape, jnp.int32),
                pltpu.VMEM((slots, tiles), jnp.int32),
                pltpu.VMEM((8, 128), jnp.int32),
                pltpu.VMEM((nz, 8, 128), jnp.int32),
                pltpu.SMEM((nz, 8, 128), jnp.int32),
                pltpu.VMEM((nz, tiles, slots, edge, edge), bf16),
                pltpu.VMEM((NY * n_xg, rest, width), bf16),
                pltpu.VMEM((NY * NX * NC, rest, width), bf16),
                pltpu.VMEM((n_yg * NX, FIRST, width), bf16),
                pltpu.VMEM((NY * NX * NC, FIRST, width), bf16),
                pltpu.VMEM((NY * NX * NC, 1, width), jnp.float32),
                pltpu.VMEM((NY, 1, width), jnp.float32),
                dma, dma((4, NY // 2)),
                dma, dma, dma((4, nz // 2)),
                dma, dma((2, nz // 2)),
                dma, dma((NX - 1,)),
                dma, dma, dma, dma, dma, dma, dma, dma,
                dma((nz,)),
                pltpu.SemaphoreType.REGULAR,
                pltpu.SemaphoreType.REGULAR,
            ]
            + [pltpu.VMEM((tiles, rest, width), bf16)] * NY
            + [pltpu.VMEM((tiles, FIRST, width), bf16)] * NX,
            compiler_params=pltpu.CompilerParams(
                collective_id=0, has_side_effects=True, vmem_limit_bytes=VMEM
            ),
            name="expand",
        )(a_tiles, block_owner.T, send_rows, stripe.reshape(tiles, edge, width))
        return out.reshape(tiles * edge, width)

    placed = (P("row", "col", None, None), P("row", "col"), P(), P("row", "col"))
    return jax.shard_map(local, mesh=mesh, in_specs=placed, out_specs=P("row", "col"), check_vma=False)
```

```python
import functools

import jax
import jax.numpy as jnp
from jax import lax
from jax.experimental import pallas as pl
from jax.experimental.pallas import tpu as pltpu
from jax.sharding import PartitionSpec as P

MESH = pl.DeviceIdType.MESH
FIRST_PLANE = (
    "o u Y1 y1", "g1 s r Y2", "y2 w g2 Z1", "x t0 z1 t1", "Y3 y3 Z2 g3", "z2 t2 Z3 Y4",
    "g4 z3 t3 Z4", "z4 Z5 z5",
)
EARLY_PLANES = (
    "o u s r", "Y1 y1 g1 w", "Y2 Z1 y2 z1", "g2 x t0 Z2", "Y3 t1 y3 z2", "g3 t2 Z3 Y4",
    "z3 g4 Z4 t3", "z4 Z5 z5",
)
LATE_PLANES = (
    "s o u r", "Y1 Z1 y1 z1", "g1 w Y2 Z2", "y2 z2 g2 x", "t0 Z3 Y3 t1", "y3 z3 g3 t2",
    "Z4 Y4 z4 g4", "Z5 t3 z5",
)
VMEM = 62 * 2**20
NX, NY, NC = 4, 8, 2
EARLY = 4
FIRST = 32


def hops_of(n):
    return [(+1, 0, n // 2), (-1, 1, n // 2), (+1, 1, n // 2 - 1), (-1, 0, n // 2 - 1)]


def ring_of(n):
    return [(+1, 0, n // 2 - 1), (-1, 1, n // 2), (+1, 1, n // 2 - 1), (-1, 0, n // 2)]


def place_of(direction, hop, n):
    return hop if direction > 0 or hop == n // 2 else n // 2 + hop


def distance_of(place, n):
    return place if place <= n // 2 else -(place - n // 2)


def kernel(nz, a_ref, owner_ref, rows_ref, stripe_ref, out_ref, rows, owners, ids_out, ids, ids_s, held, sent1, got1,
           sent2, got2, sums1, sums2, ysem, yrecv, zsem, zfirst, zrecv, isem, irecv, xsem, xrecv, s1, r1, s2, r2, c1, d1, c2, d2,
           local_sem, plane_in, ring_in, *blocks):
    yb, xb = blocks[:NY], blocks[NY:]
    me, z = lax.axis_index("row"), lax.axis_index("col")
    y, x, c = lax.div(me, NX * NC), lax.rem(lax.div(me, NC), NX), lax.rem(me, NC)

    def row(dy, dx, dc):
        return lax.rem(y + (dy + NY), NY) * (NX * NC) + lax.rem(x + (dx + NX), NX) * NC + lax.rem(c + dc, NC)

    def at(dy=0, dx=0, dc=0, dz=0):
        return (row(dy, dx, dc), lax.rem(z + (dz + nz), nz) if dz else z)

    tiles, edge, width = stripe_ref.shape
    rest = edge - FIRST
    xg = [(dx, dc) for dx in (2, 1, 3, 0) for dc in range(NC) if dx or dc]
    yg = [(dy, dc) for dy in (0, 1, 7, 2, 6, 3, 5, 4) for dc in range(NC) if dy or dc]

    own = [
        pltpu.make_async_copy(rows_ref, rows, local_sem.at[0]),
        pltpu.make_async_copy(stripe_ref.at[:, pl.ds(FIRST, rest)], yb[0], local_sem.at[1]),
        pltpu.make_async_copy(stripe_ref.at[:, pl.ds(0, FIRST)], xb[0], local_sem.at[2]),
        pltpu.make_async_copy(a_ref, held.at[0], local_sem.at[3]),
        pltpu.make_async_copy(owner_ref, owners, local_sem.at[4]),
    ]
    for copy in own:
        copy.start()

    barrier = pltpu.get_barrier_semaphore()

    def tell(dz, dy, dx, core):
        there, level = at(dy, dx, 0, dz)
        pl.semaphore_signal(barrier, inc=1, device_id=(there - c + core, level), device_id_type=MESH)

    plane = [(1, 0), (-1, 0)] + [(0, dx) for dx in range(1, NX)]
    for dy, dx in plane:
        tell(0, dy, dx, 0)
    tell(1, 0, 0, 1)
    tell(-1, 0, 0, 1)

    @pl.when(c == 1)
    def _():
        tell(0, 0, 0, 0)

    ids_out[...] = jnp.zeros_like(ids_out)
    own.pop().wait()
    ids_out[0 : owners.shape[0], 0 : owners.shape[1]] = owners[...]
    ids[0] = ids_out[...]

    @pl.when(c == 0)
    def _():
        pl.semaphore_wait(barrier, 2 * len(plane) + 1)
        pl.semaphore_signal(plane_in, inc=1, device_id=at(dc=1), device_id_type=MESH)

    @pl.when(c == 1)
    def _():
        pl.semaphore_wait(plane_in, 1)

    def meet_ring():
        @pl.when(c == 1)
        def _():
            pl.semaphore_wait(barrier, 4)
            pl.semaphore_signal(ring_in, inc=1, device_id=at(dc=1), device_id_type=MESH)

        @pl.when(c == 0)
        def _():
            pl.semaphore_wait(ring_in, 1)

    def remote(src, dst, send_sem, recv_sem, device):
        return pltpu.make_async_remote_copy(
            src_ref=src, dst_ref=dst, send_sem=send_sem, recv_sem=recv_sem, device_id=device, device_id_type=MESH
        )

    half = tiles // 2

    def y_copy(lane, hop):
        direction, chunk, _ = hops_of(NY)[lane]
        part = pl.ds(chunk * half, half)
        if hop == 0:
            src = stripe_ref.at[part, pl.ds(FIRST, rest)]
        else:
            src = yb[place_of(direction, hop, NY)].at[part]
        dst = yb[place_of(direction, hop + 1, NY)].at[part]
        return remote(src, dst, ysem, yrecv.at[lane, hop], at(dy=direction))

    def z_copy(lane, hop):
        direction, chunk, _ = ring_of(nz)[lane]
        part = pl.ds(chunk * half, half)
        src = a_ref.at[part] if hop == 0 else held.at[place_of(direction, hop, nz), part]
        dst = held.at[place_of(direction, hop + 1, nz), part]
        return remote(src, dst, zfirst if hop == 0 and lane < 2 else zsem, zrecv.at[lane, hop], at(dz=direction))

    def i_copy(lane, hop):
        direction = ring_of(nz)[lane][0]
        src = ids_out if hop == 0 else ids.at[place_of(direction, hop, nz)]
        dst = ids.at[place_of(direction, hop + 1, nz)]
        return remote(src, dst, isem, irecv.at[lane, hop], at(dz=direction))

    def arrive(copy_of, lane, hop, last):
        if hop <= last:
            copy_of(lane, hop - 1).wait_recv()
            if hop < last:
                copy_of(lane, hop).start()

    def slot1(k):
        return jnp.where(k > NY // 2, 2 * (NY - k), jnp.maximum(2 * k - 1, 0))

    def give1(hop):
        places = [place_of(1, hop, NY)] + ([place_of(-1, hop, NY)] if 0 < hop < NY // 2 else [])
        first = max(2 * hop - 1, 0)
        owners_y = [row(-distance_of(place, NY), 0, 0) for place in places]
        mine = (x * NC + c) * NY + first
        for n, (dx, dc) in enumerate(xg):
            there = row(0, dx, dc)
            for k, (place, owner) in enumerate(zip(places, owners_y)):
                sent1[n * NY + first + k] = yb[place][rows[owner, there]]
            remote(sent1.at[pl.ds(n * NY + first, len(places))], got1.at[pl.ds(mine, len(places))], s1, r1,
                   at(0, dx, dc)).start()
        for k, (place, owner) in enumerate(zip(places, owners_y)):
            got1[mine + k] = yb[place][rows[owner, me]]

    def from_x(dx):
        return row(0, dx, 0)

    def slot2(yy, xx, cc):
        return (yy * NC + cc) * NX + xx

    def give2(first, stop):
        for n, (dy, dc) in list(enumerate(yg))[first:stop]:
            there = row(dy, 0, dc)
            for dx in range(NX):
                sent2[n * NX + lax.rem(x + dx, NX)] = xb[dx][rows[from_x(dx), there]]
            remote(sent2.at[pl.ds(n * NX, NX)], got2.at[pl.ds(slot2(y, 0, c), NX)], s2, r2, at(dy, 0, dc)).start()

    def x_copy(dx):
        return remote(stripe_ref.at[:, pl.ds(0, FIRST)], xb[dx], xsem, xrecv.at[dx - 1], at(dx=-dx))

    def start_ring():
        meet_ring()
        for lane in range(2):
            i_copy(lane, 0).start()
            z_copy(lane, 0).start()

    def y_step(hop, second):
        for lane in (2, 3) if second else (0, 1):
            arrive(y_copy, lane, hop, hops_of(NY)[lane][2])

    def near_copy(h):
        return pltpu.make_async_copy(ids.at[h], ids_s.at[h], local_sem.at[h])

    def z_step(hop, second):
        for lane in (2, 3) if second else (0, 1):
            last = ring_of(nz)[lane][2]
            if hop <= last:
                z_copy(lane, hop - 1).wait_recv()
            if not second:
                arrive(i_copy, lane, hop, nz // 2 - 1 + lane)
                place = place_of(ring_of(nz)[lane][0], hop, nz)
                if place != nz // 2:
                    near_copy(place).start()
            if hop < last:
                z_copy(lane, hop).start()

    def x_step():
        for dx in range(1, NX):
            x_copy(dx).wait_recv()
        for dx in range(NX):
            got2[slot2(y, lax.rem(x + dx, NX), c)] = xb[dx][rows[from_x(dx), me]]

    for lane in range(2):
        y_copy(lane, 0).start()
    for dx in range(1, NX):
        x_copy(dx).start()

    def run(order):
        for step in [step for part in order for step in part.split()]:
            kind, n = step[0], int(step[1:] or 0)
            if kind == "s":
                start_ring()
            elif kind == "w":
                pltpu.make_async_copy(held.at[0], held.at[0], zfirst).wait()
            elif kind == "r":
                z_copy(2, 0).start()
                z_copy(3, 0).start()
            elif kind == "u":
                y_copy(2, 0).start()
                y_copy(3, 0).start()
            elif kind == "o":
                for copy in own:
                    copy.wait()
                near_copy(0).start()
                give1(0)
            elif kind in "Yy":
                y_step(n, kind == "y")
            elif kind in "Zz":
                z_step(n, kind == "z")
            elif kind == "x":
                x_step()
            elif kind == "t":
                give2(*((0, 5), (5, 9), (9, 13), (13, 15))[n])
            elif kind == "g":
                give1(n)

    @pl.when(z == 0)
    def _():
        run(FIRST_PLANE)

    @pl.when((z > 0) & (z < EARLY))
    def _():
        run(EARLY_PLANES)

    @pl.when(z >= EARLY)
    def _():
        run(LATE_PLANES)

    n1, n2 = NY * len(xg), len(yg) * NX
    far = nz // 2
    for h in range(nz):
        if h != far:
            near_copy(h).wait()
    pltpu.make_async_copy(got2.at[pl.ds(0, n2)], got2.at[pl.ds(0, n2)], r2).wait()
    pltpu.make_async_copy(got1.at[pl.ds(0, n1)], got1.at[pl.ds(0, n1)], r1).wait()

    def partial(p, blocks_of_a):
        acc = jnp.zeros((edge, width), jnp.float32)
        for h in blocks_of_a:
            parts = []
            for s in range(2):
                o = ids_s[h, s, p]
                oy, ox, oc = o >> 3, (o >> 1) & 3, o & 1
                parts += [got2[slot2(oy, ox, oc)], got1[(ox * NC + oc) * NY + slot1((y - oy) & (NY - 1))]]
            left = jnp.concatenate([held[h, p, 0], held[h, p, 1]], axis=1)
            acc += jnp.dot(left, jnp.concatenate(parts, axis=0), preferred_element_type=jnp.float32)
        return acc

    def most(p, _):
        out_ref[p] = partial(p, [h for h in range(nz) if h != far])
        return 0

    lax.fori_loop(0, tiles, most, 0)
    i_copy(1, far - 1).wait_recv()
    copy = pltpu.make_async_copy(ids.at[far], ids_s.at[far], local_sem.at[far])
    copy.start()
    for lane in (1, 3):
        z_copy(lane, far - 1).wait_recv()
    copy.wait()

    def finish(p, total):
        acc = out_ref[p] + partial(p, [far])
        squared = acc * acc
        out_ref[p] = squared
        return total + jnp.sum(squared.reshape(edge // 8, 8, width), axis=0)

    total = lax.fori_loop(0, tiles, finish, jnp.zeros((8, width), jnp.float32))

    sums1[0] = jnp.sum(total, axis=0, keepdims=True)
    far_first = sorted(
        ((dy, dx, dc) for dy in range(NY) for dx in range(NX) for dc in range(NC) if dy or dx or dc),
        key=lambda o: -min(o[0], NY - o[0]) - min(o[1], NX - o[1]),
    )
    for n, (dy, dx, dc) in enumerate(far_first):
        remote(sums1.at[0], sums1.at[n + 1], c1, d1, at(dy, dx, dc)).start()
    pltpu.make_async_copy(sums1.at[pl.ds(1, len(far_first))], sums1.at[pl.ds(1, len(far_first))], d1).wait()
    column_sum = jnp.sum(sums1[...], axis=0)
    row_count = float(NY * NX * NC * tiles * edge)

    def scale(p, _):
        out_ref[p] = row_count * out_ref[p] / column_sum
        return 0

    lax.fori_loop(0, tiles, scale, 0)

    for ref, sem in (
        (sent1, s1), (sent2, s2), (sums1.at[pl.ds(1, len(far_first))], c1),
        (sent1.at[pl.ds(0, (NY - 1) * tiles)], ysem), (sent2.at[pl.ds(0, (NX - 1) * tiles)], xsem),
        (held.at[pl.ds(1, nz - 2)], zsem), (ids.at[pl.ds(1, nz - 1)], isem),
    ):
        pltpu.make_async_copy(ref, ref, sem).wait()


def solution(mesh):
    nz = mesh.shape["col"]
    n_xg, n_yg = NX * NC - 1, NY * NC - 1

    def local(a_tiles, block_owner, send_rows, stripe):
        tiles, slots, edge, _ = a_tiles.shape
        width = stripe.shape[1]
        rest = edge - FIRST
        vmem, hbm = pl.BlockSpec(memory_space=pltpu.VMEM), pl.BlockSpec(memory_space=pltpu.MemorySpace.HBM)
        dma, bf16 = pltpu.SemaphoreType.DMA, jnp.bfloat16
        out = pl.pallas_call(
            functools.partial(kernel, nz),
            out_shape=pltpu.VMEM((tiles, edge, width), jnp.float32),
            in_specs=[hbm, hbm, hbm, hbm],
            out_specs=vmem,
            scratch_shapes=[
                pltpu.SMEM(send_rows.shape, jnp.int32),
                pltpu.VMEM((slots, tiles), jnp.int32),
                pltpu.VMEM((8, 128), jnp.int32),
                pltpu.VMEM((nz, 8, 128), jnp.int32),
                pltpu.SMEM((nz, 8, 128), jnp.int32),
                pltpu.VMEM((nz, tiles, slots, edge, edge), bf16),
                pltpu.VMEM((NY * n_xg, rest, width), bf16),
                pltpu.VMEM((NY * NX * NC, rest, width), bf16),
                pltpu.VMEM((n_yg * NX, FIRST, width), bf16),
                pltpu.VMEM((NY * NX * NC, FIRST, width), bf16),
                pltpu.VMEM((NY * NX * NC, 1, width), jnp.float32),
                pltpu.VMEM((NY, 1, width), jnp.float32),
                dma, dma((4, NY // 2)),
                dma, dma, dma((4, nz // 2)),
                dma, dma((2, nz // 2)),
                dma, dma((NX - 1,)),
                dma, dma, dma, dma, dma, dma, dma, dma,
                dma((nz,)),
                pltpu.SemaphoreType.REGULAR,
                pltpu.SemaphoreType.REGULAR,
            ]
            + [pltpu.VMEM((tiles, rest, width), bf16)] * NY
            + [pltpu.VMEM((tiles, FIRST, width), bf16)] * NX,
            compiler_params=pltpu.CompilerParams(
                collective_id=0, has_side_effects=True, vmem_limit_bytes=VMEM
            ),
            name="expand",
        )(a_tiles, block_owner.T, send_rows, stripe.reshape(tiles, edge, width))
        return out.reshape(tiles * edge, width)

    placed = (P("row", "col", None, None), P("row", "col"), P(), P("row", "col"))
    return jax.shard_map(local, mesh=mesh, in_specs=placed, out_specs=P("row", "col"), check_vma=False)
```

```python
import functools

import jax
import jax.numpy as jnp
from jax import lax
from jax.experimental import pallas as pl
from jax.experimental.pallas import tpu as pltpu
from jax.sharding import PartitionSpec as P

MESH = pl.DeviceIdType.MESH
FIRST_PLANE = (
    "o u Y1 y1", "g1 s r Y2", "y2 w g2 Z1", "x t0 z1 Y3", "t1 y3 Z2 g3", "z2 t2 Z3 Y4", "z3 g4 Z4 t3", "z4 Z5 z5",
)
EARLY_PLANES = (
    "o u s r", "Y1 y1 g1 w", "Y2 Z1 y2 z1", "g2 x t0 Z2", "Y3 t1 y3 z2", "g3 t2 Z3 Y4",
    "z3 g4 Z4 t3", "z4 Z5 z5",
)
LATE_PLANES = (
    "s o u r", "Y1 Z1 y1 z1", "g1 w Y2 Z2", "y2 z2 g2 x", "t0 Z3 Y3 t1", "y3 z3 g3 t2",
    "Z4 Y4 z4 g4", "Z5 t3 z5",
)
VMEM = 62 * 2**20
NX, NY, NC = 4, 8, 2
EARLY = 4
FIRST = 32


def hops_of(n):
    return [(+1, 0, n // 2), (-1, 1, n // 2), (+1, 1, n // 2 - 1), (-1, 0, n // 2 - 1)]


def ring_of(n):
    return [(+1, 0, n // 2 - 1), (-1, 1, n // 2), (+1, 1, n // 2 - 1), (-1, 0, n // 2)]


def place_of(direction, hop, n):
    return hop if direction > 0 or hop == n // 2 else n // 2 + hop


def distance_of(place, n):
    return place if place <= n // 2 else -(place - n // 2)


def kernel(nz, a_ref, owner_ref, rows_ref, stripe_ref, out_ref, rows, owners, ids_out, ids, ids_s, held, sent1, got1,
           sent2, got2, sums1, sums2, ysem, yrecv, zsem, zfirst, zrecv, isem, irecv, xsem, xrecv, s1, r1, s2, r2, c1, d1, c2, d2,
           local_sem, plane_in, ring_in, *blocks):
    yb, xb = blocks[:NY], blocks[NY:]
    me, z = lax.axis_index("row"), lax.axis_index("col")
    y, x, c = lax.div(me, NX * NC), lax.rem(lax.div(me, NC), NX), lax.rem(me, NC)

    def row(dy, dx, dc):
        return lax.rem(y + (dy + NY), NY) * (NX * NC) + lax.rem(x + (dx + NX), NX) * NC + lax.rem(c + dc, NC)

    def at(dy=0, dx=0, dc=0, dz=0):
        return (row(dy, dx, dc), lax.rem(z + (dz + nz), nz) if dz else z)

    tiles, edge, width = stripe_ref.shape
    rest = edge - FIRST
    xg = [(dx, dc) for dx in (2, 1, 3, 0) for dc in range(NC) if dx or dc]
    yg = [(dy, dc) for dy in (0, 1, 7, 2, 6, 3, 5, 4) for dc in range(NC) if dy or dc]

    own = [
        pltpu.make_async_copy(rows_ref, rows, local_sem.at[0]),
        pltpu.make_async_copy(stripe_ref.at[:, pl.ds(FIRST, rest)], yb[0], local_sem.at[1]),
        pltpu.make_async_copy(stripe_ref.at[:, pl.ds(0, FIRST)], xb[0], local_sem.at[2]),
        pltpu.make_async_copy(a_ref, held.at[0], local_sem.at[3]),
        pltpu.make_async_copy(owner_ref, owners, local_sem.at[4]),
    ]
    for copy in own:
        copy.start()

    barrier = pltpu.get_barrier_semaphore()

    def tell(dz, dy, dx, core):
        there, level = at(dy, dx, 0, dz)
        pl.semaphore_signal(barrier, inc=1, device_id=(there - c + core, level), device_id_type=MESH)

    plane = [(1, 0), (-1, 0)] + [(0, dx) for dx in range(1, NX)]
    for dy, dx in plane:
        tell(0, dy, dx, 0)
    tell(1, 0, 0, 1)
    tell(-1, 0, 0, 1)

    @pl.when(c == 1)
    def _():
        tell(0, 0, 0, 0)

    ids_out[...] = jnp.zeros_like(ids_out)
    own.pop().wait()
    ids_out[0 : owners.shape[0], 0 : owners.shape[1]] = owners[...]
    ids[0] = ids_out[...]

    @pl.when(c == 0)
    def _():
        pl.semaphore_wait(barrier, 2 * len(plane) + 1)
        pl.semaphore_signal(plane_in, inc=1, device_id=at(dc=1), device_id_type=MESH)

    @pl.when(c == 1)
    def _():
        pl.semaphore_wait(plane_in, 1)

    def meet_ring():
        @pl.when(c == 1)
        def _():
            pl.semaphore_wait(barrier, 4)
            pl.semaphore_signal(ring_in, inc=1, device_id=at(dc=1), device_id_type=MESH)

        @pl.when(c == 0)
        def _():
            pl.semaphore_wait(ring_in, 1)

    def remote(src, dst, send_sem, recv_sem, device):
        return pltpu.make_async_remote_copy(
            src_ref=src, dst_ref=dst, send_sem=send_sem, recv_sem=recv_sem, device_id=device, device_id_type=MESH
        )

    half = tiles // 2

    def y_copy(lane, hop):
        direction, chunk, _ = hops_of(NY)[lane]
        part = pl.ds(chunk * half, half)
        if hop == 0:
            src = stripe_ref.at[part, pl.ds(FIRST, rest)]
        else:
            src = yb[place_of(direction, hop, NY)].at[part]
        dst = yb[place_of(direction, hop + 1, NY)].at[part]
        return remote(src, dst, ysem, yrecv.at[lane, hop], at(dy=direction))

    def z_copy(lane, hop):
        direction, chunk, _ = ring_of(nz)[lane]
        part = pl.ds(chunk * half, half)
        src = a_ref.at[part] if hop == 0 else held.at[place_of(direction, hop, nz), part]
        dst = held.at[place_of(direction, hop + 1, nz), part]
        return remote(src, dst, zfirst if hop == 0 and lane < 2 else zsem, zrecv.at[lane, hop], at(dz=direction))

    def i_copy(lane, hop):
        direction = ring_of(nz)[lane][0]
        src = ids_out if hop == 0 else ids.at[place_of(direction, hop, nz)]
        dst = ids.at[place_of(direction, hop + 1, nz)]
        return remote(src, dst, isem, irecv.at[lane, hop], at(dz=direction))

    def arrive(copy_of, lane, hop, last):
        if hop <= last:
            copy_of(lane, hop - 1).wait_recv()
            if hop < last:
                copy_of(lane, hop).start()

    def slot1(k):
        return jnp.where(k > NY // 2, 2 * (NY - k), jnp.maximum(2 * k - 1, 0))

    def give1(hop):
        places = [place_of(1, hop, NY)] + ([place_of(-1, hop, NY)] if 0 < hop < NY // 2 else [])
        first = max(2 * hop - 1, 0)
        owners_y = [row(-distance_of(place, NY), 0, 0) for place in places]
        mine = (x * NC + c) * NY + first
        for n, (dx, dc) in enumerate(xg):
            there = row(0, dx, dc)
            for k, (place, owner) in enumerate(zip(places, owners_y)):
                sent1[n * NY + first + k] = yb[place][rows[owner, there]]
            remote(sent1.at[pl.ds(n * NY + first, len(places))], got1.at[pl.ds(mine, len(places))], s1, r1,
                   at(0, dx, dc)).start()
        for k, (place, owner) in enumerate(zip(places, owners_y)):
            got1[mine + k] = yb[place][rows[owner, me]]

    def from_x(dx):
        return row(0, dx, 0)

    def slot2(yy, xx, cc):
        return (yy * NC + cc) * NX + xx

    def give2(first, stop):
        for n, (dy, dc) in list(enumerate(yg))[first:stop]:
            there = row(dy, 0, dc)
            for dx in range(NX):
                sent2[n * NX + lax.rem(x + dx, NX)] = xb[dx][rows[from_x(dx), there]]
            remote(sent2.at[pl.ds(n * NX, NX)], got2.at[pl.ds(slot2(y, 0, c), NX)], s2, r2, at(dy, 0, dc)).start()

    def x_copy(dx):
        return remote(stripe_ref.at[:, pl.ds(0, FIRST)], xb[dx], xsem, xrecv.at[dx - 1], at(dx=-dx))

    def start_ring():
        meet_ring()
        for lane in range(2):
            i_copy(lane, 0).start()
            z_copy(lane, 0).start()

    def y_step(hop, second):
        for lane in (2, 3) if second else (0, 1):
            arrive(y_copy, lane, hop, hops_of(NY)[lane][2])

    def near_copy(h):
        return pltpu.make_async_copy(ids.at[h], ids_s.at[h], local_sem.at[h])

    def z_step(hop, second):
        for lane in (2, 3) if second else (0, 1):
            last = ring_of(nz)[lane][2]
            if hop <= last:
                z_copy(lane, hop - 1).wait_recv()
            if not second:
                arrive(i_copy, lane, hop, nz // 2 - 1 + lane)
                place = place_of(ring_of(nz)[lane][0], hop, nz)
                if place != nz // 2:
                    near_copy(place).start()
            if hop < last:
                z_copy(lane, hop).start()

    def x_step():
        for dx in range(1, NX):
            x_copy(dx).wait_recv()
        for dx in range(NX):
            got2[slot2(y, lax.rem(x + dx, NX), c)] = xb[dx][rows[from_x(dx), me]]

    for lane in range(2):
        y_copy(lane, 0).start()
    for dx in range(1, NX):
        x_copy(dx).start()

    def run(order):
        for step in [step for part in order for step in part.split()]:
            kind, n = step[0], int(step[1:] or 0)
            if kind == "s":
                start_ring()
            elif kind == "w":
                pltpu.make_async_copy(held.at[0], held.at[0], zfirst).wait()
            elif kind == "r":
                z_copy(2, 0).start()
                z_copy(3, 0).start()
            elif kind == "u":
                y_copy(2, 0).start()
                y_copy(3, 0).start()
            elif kind == "o":
                for copy in own:
                    copy.wait()
                near_copy(0).start()
                give1(0)
            elif kind in "Yy":
                y_step(n, kind == "y")
            elif kind in "Zz":
                z_step(n, kind == "z")
            elif kind == "x":
                x_step()
            elif kind == "t":
                give2(*((0, 5), (5, 9), (9, 13), (13, 15))[n])
            elif kind == "g":
                give1(n)

    @pl.when(z == 0)
    def _():
        run(FIRST_PLANE)

    @pl.when((z > 0) & (z < EARLY))
    def _():
        run(EARLY_PLANES)

    @pl.when(z >= EARLY)
    def _():
        run(LATE_PLANES)

    n1, n2 = NY * len(xg), len(yg) * NX
    far = nz // 2
    for h in range(nz):
        if h != far:
            near_copy(h).wait()
    pltpu.make_async_copy(got2.at[pl.ds(0, n2)], got2.at[pl.ds(0, n2)], r2).wait()
    pltpu.make_async_copy(got1.at[pl.ds(0, n1)], got1.at[pl.ds(0, n1)], r1).wait()

    def partial(p, blocks_of_a):
        acc = jnp.zeros((edge, width), jnp.float32)
        for h in blocks_of_a:
            parts = []
            for s in range(2):
                o = ids_s[h, s, p]
                oy, ox, oc = o >> 3, (o >> 1) & 3, o & 1
                parts += [got2[slot2(oy, ox, oc)], got1[(ox * NC + oc) * NY + slot1((y - oy) & (NY - 1))]]
            left = jnp.concatenate([held[h, p, 0], held[h, p, 1]], axis=1)
            acc += jnp.dot(left, jnp.concatenate(parts, axis=0), preferred_element_type=jnp.float32)
        return acc

    def most(p, _):
        out_ref[p] = partial(p, [h for h in range(nz) if h != far])
        return 0

    lax.fori_loop(0, tiles, most, 0)
    i_copy(1, far - 1).wait_recv()
    copy = pltpu.make_async_copy(ids.at[far], ids_s.at[far], local_sem.at[far])
    copy.start()
    for lane in (1, 3):
        z_copy(lane, far - 1).wait_recv()
    copy.wait()

    def finish(p, total):
        acc = out_ref[p] + partial(p, [far])
        squared = acc * acc
        out_ref[p] = squared
        return total + jnp.sum(squared.reshape(edge // 8, 8, width), axis=0)

    total = lax.fori_loop(0, tiles, finish, jnp.zeros((8, width), jnp.float32))

    sums1[0] = jnp.sum(total, axis=0, keepdims=True)
    far_first = sorted(
        ((dy, dx, dc) for dy in range(NY) for dx in range(NX) for dc in range(NC) if dy or dx or dc),
        key=lambda o: -min(o[0], NY - o[0]) - min(o[1], NX - o[1]),
    )
    for n, (dy, dx, dc) in enumerate(far_first):
        remote(sums1.at[0], sums1.at[n + 1], c1, d1, at(dy, dx, dc)).start()
    pltpu.make_async_copy(sums1.at[pl.ds(1, len(far_first))], sums1.at[pl.ds(1, len(far_first))], d1).wait()
    column_sum = jnp.sum(sums1[...], axis=0)
    row_count = float(NY * NX * NC * tiles * edge)

    def scale(p, _):
        out_ref[p] = row_count * out_ref[p] / column_sum
        return 0

    lax.fori_loop(0, tiles, scale, 0)

    for ref, sem in (
        (sent1, s1), (sent2, s2), (sums1.at[pl.ds(1, len(far_first))], c1),
        (sent1.at[pl.ds(0, (NY - 1) * tiles)], ysem), (sent2.at[pl.ds(0, (NX - 1) * tiles)], xsem),
        (held.at[pl.ds(1, nz - 2)], zsem), (ids.at[pl.ds(1, nz - 1)], isem),
    ):
        pltpu.make_async_copy(ref, ref, sem).wait()


def solution(mesh):
    nz = mesh.shape["col"]
    n_xg, n_yg = NX * NC - 1, NY * NC - 1

    def local(a_tiles, block_owner, send_rows, stripe):
        tiles, slots, edge, _ = a_tiles.shape
        width = stripe.shape[1]
        rest = edge - FIRST
        vmem, hbm = pl.BlockSpec(memory_space=pltpu.VMEM), pl.BlockSpec(memory_space=pltpu.MemorySpace.HBM)
        dma, bf16 = pltpu.SemaphoreType.DMA, jnp.bfloat16
        out = pl.pallas_call(
            functools.partial(kernel, nz),
            out_shape=pltpu.VMEM((tiles, edge, width), jnp.float32),
            in_specs=[hbm, hbm, hbm, hbm],
            out_specs=vmem,
            scratch_shapes=[
                pltpu.SMEM(send_rows.shape, jnp.int32),
                pltpu.VMEM((slots, tiles), jnp.int32),
                pltpu.VMEM((8, 128), jnp.int32),
                pltpu.VMEM((nz, 8, 128), jnp.int32),
                pltpu.SMEM((nz, 8, 128), jnp.int32),
                pltpu.VMEM((nz, tiles, slots, edge, edge), bf16),
                pltpu.VMEM((NY * n_xg, rest, width), bf16),
                pltpu.VMEM((NY * NX * NC, rest, width), bf16),
                pltpu.VMEM((n_yg * NX, FIRST, width), bf16),
                pltpu.VMEM((NY * NX * NC, FIRST, width), bf16),
                pltpu.VMEM((NY * NX * NC, 1, width), jnp.float32),
                pltpu.VMEM((NY, 1, width), jnp.float32),
                dma, dma((4, NY // 2)),
                dma, dma, dma((4, nz // 2)),
                dma, dma((2, nz // 2)),
                dma, dma((NX - 1,)),
                dma, dma, dma, dma, dma, dma, dma, dma,
                dma((nz,)),
                pltpu.SemaphoreType.REGULAR,
                pltpu.SemaphoreType.REGULAR,
            ]
            + [pltpu.VMEM((tiles, rest, width), bf16)] * NY
            + [pltpu.VMEM((tiles, FIRST, width), bf16)] * NX,
            compiler_params=pltpu.CompilerParams(
                collective_id=0, has_side_effects=True, vmem_limit_bytes=VMEM
            ),
            name="expand",
        )(a_tiles, block_owner.T, send_rows, stripe.reshape(tiles, edge, width))
        return out.reshape(tiles * edge, width)

    placed = (P("row", "col", None, None), P("row", "col"), P(), P("row", "col"))
    return jax.shard_map(local, mesh=mesh, in_specs=placed, out_specs=P("row", "col"), check_vma=False)
```
